256 devices in a mesh: res: 16 (over x, y_lo, core), seq: 16 (over y_hi, z).
Axes of the slice: x: 4, y: 4 (y_hi: 2, y_lo: 2; y = y_hi * 2 + y_lo), z: 8, core: 2. Of those that a mesh axis runs over, the one named last changes fastest.
Arguments:
- alignment_embedding: bfloat16 [512, 1024, 256], P('seq', 'res'), may hold values from -6 to 6
- standardizer_scaling: float32 [256], replicated, may hold values from 0.1 to 1.9
- standardizer_offset: float32 [256], replicated, may hold values from -1 to 1
- first_map_matrix: bfloat16 [256, 32], replicated, may hold values from -0.375 to 0.375
- first_map_offset: float32 [32], replicated, may hold values from -0.6 to 0.6
- second_map_matrix: bfloat16 [256, 32], replicated, may hold values from -0.375 to 0.375
- second_map_offset: float32 [32], replicated, may hold values from -0.6 to 0.6
- final_map_matrix: bfloat16 [1024, 128], replicated, may hold values from -4 to 4
- final_map_offset: float32 [128], replicated, may hold values from -2 to 2
Outputs:
- pair_update: bfloat16 [1024, 1024, 128], P('res', 'seq')
The draws below stay inside these ranges and needn't reach their ends.
All inputs are finite; a program needn't handle non-finite values.
Results may differ from the reference program's by a relative error of at most 0.0059.
Values may be sent and summed in bfloat16 or wider, within the bound.
A program may use at most 128 MiB of HBM per device.

```python
import jax
import jax.numpy as jnp
from jax import lax

ALIGN_FEATURES = 256
HIDDEN_WIDTH = 32
CZ = 128
ALIGNED_ROWS = 512
POSITION_TOTAL = 1024


def block_scale(stream_key, shape, shards, smallest, largest):
    def one(dim, parts):
        draws = jax.random.uniform(jax.random.fold_in(jax.random.fold_in(stream_key, 6), dim), (parts,), jnp.float32, smallest / len(shards), largest / len(shards))
        return jnp.repeat(jnp.exp(draws), shape[dim] // parts).reshape((-1,) + (1,) * (len(shape) - dim - 1))

    loudness = one(*shards[0])
    for cut in shards[1:]:
        loudness = loudness * one(*cut)
    return loudness


def centred(stream_key, extent, deviation, reach, split=(), kind=jnp.bfloat16):
    entries = jax.random.normal(stream_key, extent, jnp.float32) * deviation
    if len(split) > 0:
        entries = block_scale(stream_key, extent, split, -0.22, 0.18) * entries
    return jnp.clip(entries, min=-reach, max=reach).astype(kind)


def setup_inputs(seed: int = 0) -> dict:
    arg_keys = jax.random.split(jax.random.key(seed), 10)
    return {
        "alignment_embedding": centred(arg_keys[0], (ALIGNED_ROWS, POSITION_TOTAL, ALIGN_FEATURES), 1.0, 6.0, ((0, 16), (1, 16))),
        "standardizer_scaling": jnp.clip(1.0 + 0.18 * jax.random.normal(arg_keys[1], (ALIGN_FEATURES,), jnp.float32), 0.1, 1.9),
        "standardizer_offset": centred(arg_keys[2], (ALIGN_FEATURES,), 0.2, 1.0, (), jnp.float32),
        "first_map_matrix": centred(arg_keys[3], (ALIGN_FEATURES, HIDDEN_WIDTH), ALIGN_FEATURES ** -0.5, 0.375),
        "first_map_offset": centred(arg_keys[4], (HIDDEN_WIDTH,), 0.15, 0.6, (), jnp.float32),
        "second_map_matrix": centred(arg_keys[5], (ALIGN_FEATURES, HIDDEN_WIDTH), ALIGN_FEATURES ** -0.5, 0.375),
        "second_map_offset": centred(arg_keys[6], (HIDDEN_WIDTH,), 0.15, 0.6, (), jnp.float32),
        "final_map_matrix": centred(arg_keys[7], (HIDDEN_WIDTH * HIDDEN_WIDTH, CZ), 0.7, 4.0),
        "final_map_offset": centred(arg_keys[8], (CZ,), 0.5, 2.0, (), jnp.float32),
    }


def standardize_features(values, standardizer_scaling, standardizer_offset):
    values = values.astype(jnp.float32)
    center = lax.optimization_barrier(jnp.mean(values, axis=-1, keepdims=True))
    spread = lax.optimization_barrier(jnp.mean((values - center) ** 2, axis=-1, keepdims=True))
    return (values - center) * lax.rsqrt(spread + 1e-05) * standardizer_scaling + standardizer_offset

def linear_map_half(standardized_alignment, coefficient_matrix, offset_vector):
    input_lines = standardized_alignment.reshape(-1, standardized_alignment.shape[-1])
    return (jnp.dot(input_lines, coefficient_matrix, preferred_element_type=jnp.float32) + offset_vector).astype(jnp.bfloat16)

def reference(alignment_embedding, standardizer_scaling, standardizer_offset, first_map_matrix, first_map_offset, second_map_matrix, second_map_offset, final_map_matrix, final_map_offset):
    standardized_alignment = standardize_features(alignment_embedding, standardizer_scaling, standardizer_offset).astype(jnp.bfloat16)
    first_factor = linear_map_half(standardized_alignment, first_map_matrix, first_map_offset).reshape(ALIGNED_ROWS, POSITION_TOTAL * HIDDEN_WIDTH)
    second_factor = linear_map_half(standardized_alignment, second_map_matrix, second_map_offset).reshape(ALIGNED_ROWS, POSITION_TOTAL * HIDDEN_WIDTH)
    width = min(64, POSITION_TOTAL)

    def one_block(index):
        start = (index * width * HIDDEN_WIDTH).astype(jnp.int32)
        piece = lax.dynamic_slice_in_dim(first_factor, start, width * HIDDEN_WIDTH, 1)
        outer = lax.dot_general(piece, second_factor, (((0,), (0,)), ((), ())), preferred_element_type=jnp.float32)
        outer_mean = (outer / ALIGNED_ROWS).astype(jnp.bfloat16)
        flat = outer_mean.reshape(width, HIDDEN_WIDTH, POSITION_TOTAL, HIDDEN_WIDTH).transpose(0, 2, 1, 3).reshape(width * POSITION_TOTAL, HIDDEN_WIDTH * HIDDEN_WIDTH)
        result = jnp.dot(flat, final_map_matrix, preferred_element_type=jnp.float32) + final_map_offset
        return result.astype(jnp.bfloat16).reshape(width, POSITION_TOTAL, CZ)
    blocks = lax.map(one_block, jnp.arange(POSITION_TOTAL // width, dtype=jnp.int32))
    return blocks.reshape(POSITION_TOTAL, POSITION_TOTAL, CZ)
```

```python
import jax
import jax.numpy as jnp
from jax import lax
from jax.experimental import pallas as pl
from jax.experimental.pallas import tpu as pltpu
from jax.sharding import PartitionSpec as P

MESH = pl.DeviceIdType.MESH
BF16, F32 = jnp.bfloat16, jnp.float32
SEQS, POS, CH, HID, CZ = 32, 64, 256, 32, 128
NQ = 16
PARTS = 4
PI = POS // PARTS
LANES = PI * HID
PIECES = 8
TOTAL = SEQS * NQ


def device(x, yl, c, h, z):
    return (x * 4 + yl * 2 + c, h * 8 + z)


def kernel(
    x_hbm, gain_hbm, shift_hbm, w1_hbm, b1_hbm, w2_hbm, b2_hbm, wf_hbm, bf_hbm, out_hbm,
    xv, gain, shift, w1, b1, w2, b2, wf, bf,
    normed0, normed1, tright, lrows, rown, rpart, lbuf, rbuf, lt, wfloat, wrows, wt, outer, obuf,
    in_sem, out_sem, lsend, lrecv, r0send, r0recv, r1send, r1recv, r2send, r2recv, r3send, r3recv,
):
    r, q = lax.axis_index("res"), lax.axis_index("seq")
    x, yl, c, h, z = r // 4, (r // 2) % 2, r % 2, q // 8, q % 8
    xp, xm, xo = (x + 1) % 4, (x + 3) % 4, (x + 2) % 4
    zp, zm = (z + 1) % 8, (z + 7) % 8
    half = (c + h + z + 1) % 2
    src_yl, src_c = (q // 2) % 2, q % 2
    piece = x * 2 + yl

    barrier = pltpu.get_barrier_semaphore()
    sources = [device(x, yl, c, h, zp), device(x, yl, c, h, zm), device(x, yl, c, 1 - h, z)]
    sources += [device(xp, yl, c, h, z), device(xm, yl, c, h, z), device(xo, yl, c, h, z)]
    sources += [device(x, 1 - yl, c, h, z), device(x, yl, 1 - c, h, z)]
    sources += [device(x, src_yl, src_c, half, k) for k in range(8)]
    for who in sources:
        pl.semaphore_signal(barrier, inc=1, device_id=who, device_id_type=MESH)

    loads = []
    for k, (src, dst) in enumerate([
        (x_hbm, xv), (gain_hbm, gain), (shift_hbm, shift), (w1_hbm, w1), (b1_hbm, b1),
        (w2_hbm, w2), (b2_hbm, b2), (wf_hbm, wf), (bf_hbm, bf),
    ]):
        loads.append(pltpu.make_async_copy(src, dst, in_sem.at[k]))
        loads[-1].start()
    for load in loads:
        load.wait()

    b2c = jnp.broadcast_to(b2[...].reshape(1, HID), (128, HID)).T
    b2c = jnp.concatenate([b2c] * 4, axis=1)
    g, o = gain[...].reshape(1, CH), shift[...].reshape(1, CH)

    def norm_step(b, _):
        v = xv[pl.ds(b * 8, 8)].reshape(8 * POS, CH).astype(F32)
        d = v - jnp.mean(v, axis=-1, keepdims=True)
        n = d * lax.rsqrt(jnp.mean(d * d, axis=-1, keepdims=True) + 1e-05) * g + o
        normed0[pl.ds(b * 512, 512), :] = n[:, :128]
        normed1[pl.ds(b * 512, 512), :] = n[:, 128:]
        t = lax.dot_general(w2[...], n.astype(BF16), (((1,), (1,)), ((), ())), preferred_element_type=F32) + b2c
        for u in range(4):
            tright[pl.ds((b * 4 + u) * HID, HID), :] = t[:, u * 128:(u + 1) * 128]
        return 0

    lax.fori_loop(0, SEQS // 8, norm_step, 0)
    low = lax.broadcasted_iota(jnp.int32, (16, 128), 1) < POS
    for t in range(HID // 2):
        a = tright[pl.ds(2 * t, 16, stride=HID), :]
        b = tright[pl.ds(2 * t + 1, 16, stride=HID), :]
        lane = (t % 2) * 128
        rown[t // 2, 0:16, lane:lane + 128] = jnp.where(low, a, pltpu.roll(b, POS, 1)).astype(BF16)
        rown[t // 2, 16:32, lane:lane + 128] = jnp.where(low, pltpu.roll(a, POS, 1), b).astype(BF16)

    pl.semaphore_wait(barrier, len(sources))

    pending = []

    def send(src, dst, ssem, rsem, who):
        copy = pltpu.make_async_remote_copy(
            src_ref=src, dst_ref=dst, send_sem=ssem, recv_sem=rsem, device_id=who, device_id_type=MESH
        )
        copy.start()
        pending.append(copy)

    def arrived(ref, sem):
        pltpu.make_async_remote_copy(
            src_ref=ref, dst_ref=ref, send_sem=sem, recv_sem=sem, device_id=device(x, yl, 1 - c, h, z),
            device_id_type=MESH,
        ).wait_recv()

    px, mx, ox = device(xp, yl, c, h, z), device(xm, yl, c, h, z), device(xo, yl, c, h, z)
    for n, (xx, who) in enumerate(((xp, px), (xm, mx), (xo, ox))):
        send(rown.at[pl.ds(2 * xx, 2)], rpart.at[x], r0send.at[n], r0recv.at[x], who)

    def scatter(n, xs, ref):
        hd = xs // 2
        for y2 in range(2):
            send(
                ref.at[y2], rbuf.at[2 * x + y2, q], r1send.at[2 * n + y2], r1recv.at[z],
                device(x, y2, (h + hd + c + 1) % 2, hd, (xs % 2) * 4 + yl * 2 + c),
            )

    scatter(0, x, rown.at[pl.ds(2 * x, 2)])

    lane4 = lax.broadcasted_iota(jnp.int32, (4 * CH, 128), 1) // HID
    row4 = lax.broadcasted_iota(jnp.int32, (4 * CH, 128), 0) // CH
    w1w = jnp.concatenate([w1[...].astype(F32).T] * 4, axis=1)
    w1w = jnp.where(lane4 == row4, jnp.concatenate([w1w] * 4, axis=0), 0.0).astype(BF16)
    b1w = jnp.concatenate([b1[...].reshape(1, HID)] * 4, axis=1)

    def chunk(side, d):
        hh = h if side == 0 else 1 - h
        return hh * 8 + (z + d + 8) % 8

    def lsend_to(p, k, idx, who):
        send(lbuf.at[p, idx], lbuf.at[p, idx], lsend.at[p, k], lrecv.at[p, idx], who)

    def lwait(p, side, d):
        idx = chunk(side, d)
        arrived(lbuf.at[p, idx], lrecv.at[p, idx])

    up, down, over = device(x, yl, c, h, zp), device(x, yl, c, h, zm), device(x, yl, c, 1 - h, z)

    for p in range(PARTS):
        for gl in range(PI // 4):
            for i4 in range(4):
                i = p * PI + gl * 4 + i4
                for lo in range(2):
                    for n, normed in enumerate((normed0, normed1)):
                        lane = i4 * CH + n * 128
                        lrows[gl * 32 + lo * 16:gl * 32 + lo * 16 + 16, lane:lane + 128] = normed[
                            pl.ds(lo * POS + i, 16, stride=2 * POS), :
                        ].astype(BF16)
        left = (jnp.dot(lrows[...], w1w, preferred_element_type=F32) + b1w).astype(BF16)
        for gl in range(PI // 4):
            lbuf[p, q, :, gl * 128:(gl + 1) * 128] = left[gl * 32:(gl + 1) * 32, :]
        lsend_to(p, 0, q, up)
        lsend_to(p, 4, q, down)
        lsend_to(p, 8, q, over)

    for n, xx in enumerate((xp, xm, xo)):
        arrived(rpart.at[xx], r0recv.at[xx])
        scatter(n + 1, xx, rpart.at[xx])

    for k in range(8):
        arrived(rbuf.at[piece, half * 8 + k], r1recv.at[k])

    def quarter(k, which):
        return rbuf.at[k, pl.ds(which * 8, 8)]

    def rsend(n, k, who):
        send(quarter(k, half), quarter(k, half), r2send.at[n], r2recv.at[k], who)

    def rsibling(n, k):
        send(quarter(k, half), quarter(k, half), r3send.at[n], r3recv.at[k], device(x, yl, 1 - c, h, z))

    def rwait(k):
        arrived(quarter(k, half), r2recv.at[k])

    rsend(0, piece, device(x, 1 - yl, c, h, z))
    rsend(1, piece, px)
    rsend(2, piece, mx)
    rsend(3, piece, ox)
    rsibling(0, piece)

    wfloat[...] = wf[...].astype(F32)
    for e in range(HID):
        wrows[(e // 2) * HID:(e // 2 + 1) * HID, (e % 2) * CZ:(e % 2 + 1) * CZ] = wfloat[pl.ds(e, HID, stride=HID), :]
    wt[...] = wrows[...].T.astype(BF16)
    bias = bf[...].reshape(1, CZ)

    def step1(p):
        lwait(p, 0, -1)
        lsend_to(p, 1, chunk(0, -1), up)
        lsend_to(p, 9, chunk(0, -1), over)
        lwait(p, 0, 1)
        lsend_to(p, 5, chunk(0, 1), down)
        lsend_to(p, 10, chunk(0, 1), over)

    def step2(p):
        lwait(p, 0, -2)
        lsend_to(p, 2, chunk(0, -2), up)
        lsend_to(p, 11, chunk(0, -2), over)
        lwait(p, 0, 2)
        lsend_to(p, 6, chunk(0, 2), down)
        lsend_to(p, 12, chunk(0, 2), over)

    def step3(p):
        lwait(p, 0, -3)
        lwait(p, 0, 3)
        if p % 2 == 0:
            lsend_to(p, 3, chunk(0, -3), up)
        else:
            lsend_to(p, 7, chunk(0, 3), down)
        lwait(p, 1, -2)
        lsend_to(p, 13, chunk(1, -2), up)
        lwait(p, 1, 2)
        lsend_to(p, 15, chunk(1, 2), down)

    def step4(p):
        lwait(p, 1, -3)
        lwait(p, 1, 3)
        if p % 2 == 1:
            lsend_to(p, 14, chunk(1, -3), up)
        else:
            lsend_to(p, 16, chunk(1, 3), down)

    def finish(p):
        for side, d in ((0, 4), (1, 0), (1, -1), (1, 1), (1, 4)):
            lwait(p, side, d)

    low2 = lax.broadcasted_iota(jnp.int32, (128, 128), 1) < POS

    def compute(p):
        for b in range(4):
            lt[:, b * 128:(b + 1) * 128] = lbuf[p, 4 * b:4 * b + 4].reshape(128, LANES).T

        def first(k, _):
            prod = jnp.dot(
                lt[...], rbuf[k].reshape(TOTAL, 256), preferred_element_type=F32
            ).astype(BF16)
            for i in range(PI):
                for t in range(2):
                    outer[i // 2, pl.ds((2 * k + t) * HID, HID), (i % 2) * 128:(i % 2 + 1) * 128] = prod[
                        i * HID:(i + 1) * HID, t * 128:(t + 1) * 128
                    ]
            return 0

        lax.fori_loop(0, PIECES, first, 0)

        def second(n, _):
            y = jnp.dot(wt[...], outer[n], preferred_element_type=F32)
            for i in range(2):
                both = jnp.where(low2, y[:CZ, i * 128:(i + 1) * 128], y[CZ:, i * 128:(i + 1) * 128]).T
                pair = (both[:POS] + both[POS:]) * (1.0 / TOTAL) + bias
                obuf[p * PI + 2 * n + i] = pair.astype(BF16)
            return 0

        lax.fori_loop(0, PI // 2, second, 0)
        copy = pltpu.make_async_copy(obuf.at[pl.ds(p * PI, PI)], out_hbm.at[pl.ds(p * PI, PI)], out_sem.at[p])
        copy.start()
        return copy

    for p in range(PARTS):
        step1(p)
    other = x * 2 + 1 - yl
    rwait(other)
    rsend(4, other, px)
    rsend(5, other, mx)
    rsend(6, other, ox)
    rsibling(1, other)
    for p in range(PARTS):
        step2(p)
    for n, xx in enumerate((xp, xm, xo)):
        rwait(xx * 2 + yl)
        rsibling(2 + n, xx * 2 + yl)
    for p in range(PARTS):
        step3(p)
    for n, xx in enumerate((xp, xm, xo)):
        rwait(xx * 2 + 1 - yl)
        rsibling(5 + n, xx * 2 + 1 - yl)
    for p in range(PARTS):
        step4(p)
    for k in range(PIECES):
        arrived(quarter(k, 1 - half), r3recv.at[k])
    stores = []
    for p in range(PARTS):
        finish(p)
        stores.append(compute(p))
    for copy in pending:
        copy.wait_send()
    for copy in stores:
        copy.wait()


def local(x, gain, shift, w1, b1, w2, b2, wf, bf):
    hbm = pl.BlockSpec(memory_space=pl.ANY)
    dma = pltpu.SemaphoreType.DMA
    return pl.pallas_call(
        kernel,
        out_shape=jax.ShapeDtypeStruct((POS, POS, CZ), BF16),
        in_specs=[hbm] * 9,
        out_specs=hbm,
        scratch_shapes=[
            pltpu.VMEM((SEQS, POS, CH), BF16), pltpu.VMEM((CH,), F32), pltpu.VMEM((CH,), F32),
            pltpu.VMEM((HID, CH), BF16), pltpu.VMEM((HID,), F32),
            pltpu.VMEM((HID, CH), BF16), pltpu.VMEM((HID,), F32),
            pltpu.VMEM((HID * HID, CZ), BF16), pltpu.VMEM((CZ,), F32),
            pltpu.VMEM((SEQS * POS, 128), F32), pltpu.VMEM((SEQS * POS, 128), F32),
            pltpu.VMEM((SEQS // 2 * HID, 128), F32),
            pltpu.VMEM((PI // 4 * SEQS, 4 * CH), BF16),
            pltpu.VMEM((PIECES, SEQS, 256), BF16),
            pltpu.VMEM((4, 2, SEQS, 256), BF16),
            pltpu.VMEM((PARTS, NQ, SEQS, LANES), BF16),
            pltpu.VMEM((PIECES, NQ, SEQS, 256), BF16),
            pltpu.VMEM((LANES, TOTAL), BF16),
            pltpu.VMEM((HID * HID, CZ), F32),
            pltpu.VMEM((HID * HID // 2, 2 * CZ), F32),
            pltpu.VMEM((2 * CZ, HID * HID // 2), BF16),
            pltpu.VMEM((PI // 2, HID * HID // 2, 256), BF16),
            pltpu.VMEM((POS, POS, CZ), BF16),
            dma((9,)), dma((PARTS,)), dma((PARTS, 17)), dma((PARTS, NQ)), dma((3,)), dma((4,)), dma((PIECES,)), dma((8,)),
            dma((7,)), dma((PIECES,)), dma((PIECES,)), dma((PIECES,)),
        ],
        compiler_params=pltpu.CompilerParams(
            collective_id=0, has_side_effects=True, vmem_limit_bytes=56 * 2**20
        ),
    )(x, gain, shift, w1.T, b1, w2.T, b2, wf, bf)


def solution(mesh):
    return jax.shard_map(
        local,
        mesh=mesh,
        in_specs=(P("seq", "res", None), P(), P(), P(), P(), P(), P(), P(), P()),
        out_specs=P("res", "seq", None),
        check_vma=False,
    )
```

```python
import functools

import jax
import jax.numpy as jnp
from jax import lax
from jax.experimental import pallas as pl
from jax.experimental.pallas import tpu as pltpu
from jax.sharding import PartitionSpec as P

MESH = pl.DeviceIdType.MESH
BF16, F32 = jnp.bfloat16, jnp.float32
SEQS, POS, CH, HID, CZ = 32, 64, 256, 32, 128
NQ = 16
OWN, SKEW, LAST = 0.2, 0.65, 2.1
PARTS = 4
PI = POS // PARTS
LANES = PI * HID
PIECES = 8
TOTAL = SEQS * NQ


def device(x, yl, c, h, z):
    return (x * 4 + yl * 2 + c, h * 8 + z)


def kernel(
    x_hbm, gain_hbm, shift_hbm, w1_hbm, b1_hbm, w2_hbm, b2_hbm, wf_hbm, bf_hbm, out,
    xv, gain, shift, w1, b1, w2, b2, wf, bf,
    normed0, normed1, tright, lrows, rown, rpart, lbuf, rbuf, lt, wfloat, wrows, wt, outer,
    in_sem, lsend, lrecv, r0send, r0recv, r1send, r1recv, r2send, r2recv, r3send, r3recv,
):
    r, q = lax.axis_index("res"), lax.axis_index("seq")
    x, yl, c, h, z = r // 4, (r // 2) % 2, r % 2, q // 8, q % 8
    xp, xm, xo = (x + 1) % 4, (x + 3) % 4, (x + 2) % 4
    zp, zm = (z + 1) % 8, (z + 7) % 8
    half = (c + h + z + 1) % 2
    src_yl, src_c = (q // 2) % 2, q % 2
    piece = x * 2 + yl

    barrier = pltpu.get_barrier_semaphore()
    sources = [device(x, yl, c, h, zp), device(x, yl, c, h, zm), device(x, yl, c, 1 - h, z)]
    sources += [device(xp, yl, c, h, z), device(xm, yl, c, h, z), device(xo, yl, c, h, z)]
    sources += [device(x, 1 - yl, c, h, z), device(x, yl, 1 - c, h, z)]
    sources += [device(x, src_yl, src_c, half, k) for k in range(8)]
    for who in sources:
        pl.semaphore_signal(barrier, inc=1, device_id=who, device_id_type=MESH)

    loads = []
    for k, (src, dst) in enumerate([
        (x_hbm, xv), (gain_hbm, gain), (shift_hbm, shift), (w1_hbm, w1), (b1_hbm, b1),
        (w2_hbm, w2), (b2_hbm, b2), (wf_hbm, wf), (bf_hbm, bf),
    ]):
        loads.append(pltpu.make_async_copy(src, dst, in_sem.at[k]))
        loads[-1].start()
    for load in loads:
        load.wait()

    b2c = jnp.broadcast_to(b2[...].reshape(1, HID), (128, HID)).T
    b2c = jnp.concatenate([b2c] * 4, axis=1)
    g, o = gain[...].reshape(1, CH), shift[...].reshape(1, CH)

    def norm_step(b, _):
        v = xv[pl.ds(b * 8, 8)].reshape(8 * POS, CH).astype(F32)
        d = v - jnp.mean(v, axis=-1, keepdims=True)
        n = d * lax.rsqrt(jnp.mean(d * d, axis=-1, keepdims=True) + 1e-05) * g + o
        normed0[pl.ds(b * 512, 512), :] = n[:, :128]
        normed1[pl.ds(b * 512, 512), :] = n[:, 128:]
        t = lax.dot_general(w2[...], n.astype(BF16), (((1,), (1,)), ((), ())), preferred_element_type=F32) + b2c
        for u in range(4):
            tright[pl.ds((b * 4 + u) * HID, HID), :] = t[:, u * 128:(u + 1) * 128]
        return 0

    lax.fori_loop(0, SEQS // 8, norm_step, 0)
    low = lax.broadcasted_iota(jnp.int32, (16, 128), 1) < POS
    for t in range(HID // 2):
        a = tright[pl.ds(2 * t, 16, stride=HID), :]
        b = tright[pl.ds(2 * t + 1, 16, stride=HID), :]
        lane = (t % 2) * 128
        rown[t // 2, 0:16, lane:lane + 128] = jnp.where(low, a, pltpu.roll(b, POS, 1)).astype(BF16)
        rown[t // 2, 16:32, lane:lane + 128] = jnp.where(low, pltpu.roll(a, POS, 1), b).astype(BF16)

    pl.semaphore_wait(barrier, len(sources))

    pending = []

    def send(src, dst, ssem, rsem, who):
        copy = pltpu.make_async_remote_copy(
            src_ref=src, dst_ref=dst, send_sem=ssem, recv_sem=rsem, device_id=who, device_id_type=MESH
        )
        copy.start()
        pending.append(copy)

    def arrived(ref, sem):
        pltpu.make_async_remote_copy(
            src_ref=ref, dst_ref=ref, send_sem=sem, recv_sem=sem, device_id=device(x, yl, 1 - c, h, z),
            device_id_type=MESH,
        ).wait_recv()

    px, mx, ox = device(xp, yl, c, h, z), device(xm, yl, c, h, z), device(xo, yl, c, h, z)
    for n, (xx, who) in enumerate(((xp, px), (xm, mx), (xo, ox))):
        send(rown.at[pl.ds(2 * xx, 2)], rpart.at[x], r0send.at[n], r0recv.at[x], who)

    def scatter(n, xs, ref):
        hd = xs // 2
        for y2 in range(2):
            send(
                ref.at[y2], rbuf.at[2 * x + y2, q], r1send.at[2 * n + y2], r1recv.at[z],
                device(x, y2, (h + hd + c + 1) % 2, hd, (xs % 2) * 4 + yl * 2 + c),
            )

    scatter(0, x, rown.at[pl.ds(2 * x, 2)])

    lane4 = lax.broadcasted_iota(jnp.int32, (4 * CH, 128), 1) // HID
    row4 = lax.broadcasted_iota(jnp.int32, (4 * CH, 128), 0) // CH
    w1w = jnp.concatenate([w1[...].astype(F32).T] * 4, axis=1)
    w1w = jnp.where(lane4 == row4, jnp.concatenate([w1w] * 4, axis=0), 0.0).astype(BF16)
    b1w = jnp.concatenate([b1[...].reshape(1, HID)] * 4, axis=1)

    def chunk(side, d):
        hh = h if side == 0 else 1 - h
        return hh * 8 + (z + d + 8) % 8

    def lsend_to(p, k, idx, who):
        send(lbuf.at[p, idx], lbuf.at[p, idx], lsend.at[p, k], lrecv.at[p, idx], who)

    def lwait(p, side, d):
        idx = chunk(side, d)
        arrived(lbuf.at[p, idx], lrecv.at[p, idx])

    up, down, over = device(x, yl, c, h, zp), device(x, yl, c, h, zm), device(x, yl, c, 1 - h, z)

    def own(p):
        for gl in range(PI // 4):
            for i4 in range(4):
                i = p * PI + gl * 4 + i4
                for lo in range(2):
                    for n, normed in enumerate((normed0, normed1)):
                        lane = i4 * CH + n * 128
                        lrows[gl * 32 + lo * 16:gl * 32 + lo * 16 + 16, lane:lane + 128] = normed[
                            pl.ds(lo * POS + i, 16, stride=2 * POS), :
                        ].astype(BF16)
        left = (jnp.dot(lrows[...], w1w, preferred_element_type=F32) + b1w).astype(BF16)
        for gl in range(PI // 4):
            lbuf[p, q, :, gl * 128:(gl + 1) * 128] = left[gl * 32:(gl + 1) * 32, :]
        lsend_to(p, 0, q, up)
        lsend_to(p, 4, q, down)
        lsend_to(p, 8, q, over)

    other = x * 2 + 1 - yl
    yld, sib = device(x, 1 - yl, c, h, z), device(x, yl, 1 - c, h, z)

    def rows(k, zz):
        return rbuf.at[k, half * 8 + zz]

    def rsend(n, k, zz, who):
        send(rows(k, zz), rows(k, zz), r2send.at[n, zz], r2recv.at[k, zz], who)

    def rwait(k, zz):
        arrived(rows(k, zz), r2recv.at[k, zz])

    def eighth(k, which):
        return rbuf.at[k, pl.ds(which * 8, 8)]

    def rsibling(n, k):
        send(eighth(k, half), eighth(k, half), r3send.at[n], r3recv.at[k], sib)

    def rgather(n, k):
        for zz in range(8):
            rwait(k, zz)
        rsibling(n, k)

    def r0():
        for n, xx in enumerate((xp, xm, xo)):
            arrived(rpart.at[xx], r0recv.at[xx])
            scatter(n + 1, xx, rpart.at[xx])

    def r1(d):
        zz = (z + d + 8) % 8
        arrived(rows(piece, zz), r1recv.at[zz])
        rsend(0, piece, zz, yld)
        rsend(1, piece, zz, px)
        rsend(2, piece, zz, mx)
        rsend(3, piece, zz, ox)

    def ryl(d):
        zz = (z + d + 8) % 8
        rwait(other, zz)
        rsend(4, other, zz, px)
        rsend(5, other, zz, mx)

    def rant(d):
        zz = (z + d + 8) % 8
        rwait(xo * 2 + yl, zz)
        rsend(6, xo * 2 + yl, zz, yld)

    def rsib():
        for k in range(PIECES):
            arrived(eighth(k, 1 - half), r3recv.at[k])

    wfloat[...] = wf[...].astype(F32)
    for e in range(HID):
        wrows[(e // 2) * HID:(e // 2 + 1) * HID, (e % 2) * CZ:(e % 2 + 1) * CZ] = wfloat[pl.ds(e, HID, stride=HID), :]
    wt[...] = wrows[...].T.astype(BF16)
    bias = bf[...].reshape(1, CZ)

    def s1(p):
        lwait(p, 0, -1)
        lsend_to(p, 1, chunk(0, -1), up)
        lsend_to(p, 9, chunk(0, -1), over)
        lwait(p, 0, 1)
        lsend_to(p, 5, chunk(0, 1), down)
        lsend_to(p, 10, chunk(0, 1), over)

    def s2(p):
        lwait(p, 0, -2)
        lsend_to(p, 2, chunk(0, -2), up)
        if p % 2 == 0:
            lsend_to(p, 11, chunk(0, -2), over)
        lwait(p, 0, 2)
        lsend_to(p, 6, chunk(0, 2), down)
        if p % 2 == 1:
            lsend_to(p, 11, chunk(0, 2), over)

    def s3(p):
        lwait(p, 0, -3)
        if p % 2 == 1:
            lsend_to(p, 3, chunk(0, -3), up)
        lwait(p, 0, 3)
        if p % 2 == 0:
            lsend_to(p, 7, chunk(0, 3), down)

    def c1(p):
        if p % 2 == 1:
            lwait(p, 1, -1)
            lsend_to(p, 12, chunk(1, -1), up)
        else:
            lwait(p, 1, 1)
            lsend_to(p, 12, chunk(1, 1), down)

    def c2(p):
        lwait(p, 1, -2)
        lsend_to(p, 13, chunk(1, -2), up)
        lwait(p, 1, 2)
        lsend_to(p, 14, chunk(1, 2), down)

    def c3(p):
        if p % 2 == 0:
            lwait(p, 1, -3)
            lsend_to(p, 15, chunk(1, -3), up)
        else:
            lwait(p, 1, 3)
            lsend_to(p, 15, chunk(1, 3), down)

    def finish(p):
        if p % 2 == 0:
            last = (1, -1), (1, 3)
        else:
            last = (1, 1), (1, -3)
        for side, d in ((0, 4), (1, 0), (1, 4)) + last:
            lwait(p, side, d)

    low2 = lax.broadcasted_iota(jnp.int32, (128, 128), 1) < POS

    def compute(stage, p):
        if stage == 0:
            for b in range(4):
                lt[:, b * 128:(b + 1) * 128] = lbuf[p, 4 * b:4 * b + 4].reshape(128, LANES).T
        if stage < 2:
            for k in range(stage * 4, stage * 4 + 4):
                prod = jnp.dot(lt[...], rbuf[k].reshape(TOTAL, 256), preferred_element_type=F32).astype(BF16)
                for i in range(PI):
                    for t in range(2):
                        outer[i // 2, (2 * k + t) * HID:(2 * k + t + 1) * HID, (i % 2) * 128:(i % 2 + 1) * 128] = prod[
                            i * HID:(i + 1) * HID, t * 128:(t + 1) * 128
                        ]
            return
        for n in range((stage - 2) * 4, (stage - 2) * 4 + 4):
            y = jnp.dot(wt[...], outer[n], preferred_element_type=F32)
            for i in range(2):
                both = jnp.where(low2, y[:CZ, i * 128:(i + 1) * 128], y[CZ:, i * 128:(i + 1) * 128]).T
                pair = (both[:POS] + both[POS:]) * (1.0 / TOTAL) + bias
                out[p * PI + 2 * n + i] = pair.astype(BF16)

    near = (0, 1, -1, 2, -2, 3, -3, 4)

    def rsibling_own(_):
        rsibling(0, piece)

    steps = []

    def plan(start, pitch, step, items):
        for n, item in enumerate(items):
            steps.append((start + pitch * n, functools.partial(step, item)))

    steps.append((3.5, r0))
    plan(6.5, 0.3, r1, near)
    plan(9.0, 0, rsibling_own, [0])
    plan(10.0, 0.4, ryl, near)
    plan(13.1, 0, lambda _: rsibling(1, other), [0])
    plan(11.0, 0.45, rant, near)
    plan(14.5, 0, lambda _: rsibling(2, xo * 2 + yl), [0])
    for n, (when, k) in enumerate(((14.6, xp * 2 + yl), (14.7, xm * 2 + yl), (17.0, xp * 2 + 1 - yl), (17.1, xm * 2 + 1 - yl), (17.6, xo * 2 + 1 - yl))):
        steps.append((when, functools.partial(rgather, 3 + n, k)))
    steps.append((18.4, rsib))
    parts = range(PARTS)
    plan(0.0, OWN, own, parts)
    plan(3.9, SKEW, s1, parts)
    plan(7.0, SKEW, s2, parts)
    plan(8.1, SKEW, c1, parts)
    plan(10.0, SKEW, s3, parts)
    plan(12.6, SKEW, c2, parts)
    plan(15.5, SKEW, c3, parts)
    plan(18.5, LAST, finish, parts)
    for n in range(4):
        plan(18.5 + 0.01 + 0.5 * n, LAST, functools.partial(compute, n), parts)
    for _, step in sorted(steps, key=lambda item: item[0]):
        step()
    for copy in pending:
        copy.wait_send()


def local(x, gain, shift, w1, b1, w2, b2, wf, bf):
    args = [pltpu.with_memory_space_constraint(a, pltpu.HBM) for a in (x, gain, shift, w1.T, b1, w2.T, b2, wf, bf)]
    dma = pltpu.SemaphoreType.DMA
    return pl.pallas_call(
        kernel,
        out_shape=jax.ShapeDtypeStruct((POS, POS, CZ), BF16),
        in_specs=[pl.BlockSpec(memory_space=pltpu.HBM)] * 9,
        out_specs=pl.BlockSpec(memory_space=pltpu.VMEM),
        scratch_shapes=[
            pltpu.VMEM((SEQS, POS, CH), BF16), pltpu.VMEM((CH,), F32), pltpu.VMEM((CH,), F32),
            pltpu.VMEM((HID, CH), BF16), pltpu.VMEM((HID,), F32),
            pltpu.VMEM((HID, CH), BF16), pltpu.VMEM((HID,), F32),
            pltpu.VMEM((HID * HID, CZ), BF16), pltpu.VMEM((CZ,), F32),
            pltpu.VMEM((SEQS * POS, 128), F32), pltpu.VMEM((SEQS * POS, 128), F32),
            pltpu.VMEM((SEQS // 2 * HID, 128), F32),
            pltpu.VMEM((PI // 4 * SEQS, 4 * CH), BF16),
            pltpu.VMEM((PIECES, SEQS, 256), BF16),
            pltpu.VMEM((4, 2, SEQS, 256), BF16),
            pltpu.VMEM((PARTS, NQ, SEQS, LANES), BF16),
            pltpu.VMEM((PIECES, NQ, SEQS, 256), BF16),
            pltpu.VMEM((LANES, TOTAL), BF16),
            pltpu.VMEM((HID * HID, CZ), F32),
            pltpu.VMEM((HID * HID // 2, 2 * CZ), F32),
            pltpu.VMEM((2 * CZ, HID * HID // 2), BF16),
            pltpu.VMEM((PI // 2, HID * HID // 2, 256), BF16),
            dma((9,)), dma((PARTS, 16)), dma((PARTS, NQ)), dma((3,)), dma((4,)), dma((PIECES,)), dma((8,)),
            dma((7, 8)), dma((PIECES, 8)), dma((PIECES,)), dma((PIECES,)),
        ],
        compiler_params=pltpu.CompilerParams(
            collective_id=0, has_side_effects=True, vmem_limit_bytes=40 * 2**20
        ),
    )(*args)


def solution(mesh):
    return jax.shard_map(
        local,
        mesh=mesh,
        in_specs=(P("seq", "res", None), P(), P(), P(), P(), P(), P(), P(), P()),
        out_specs=P("res", "seq", None),
        check_vma=False,
    )
```

```python
import functools

import jax
import jax.numpy as jnp
from jax import lax
from jax.experimental import pallas as pl
from jax.experimental.pallas import tpu as pltpu
from jax.sharding import PartitionSpec as P

MESH = pl.DeviceIdType.MESH
BF16, F32 = jnp.bfloat16, jnp.float32
SEQS, POS, CH, HID, CZ = 32, 64, 256, 32, 128
NQ = 16
CROSS = (0, 0, 0, 0)
RG = 2
PARTS = 4
PI = POS // PARTS
LANES = PI * HID
GROUPS = 1
GI = POS // GROUPS
PIECES = 8
TOTAL = SEQS * NQ


def device(x, yl, c, h, z):
    return (x * 4 + yl * 2 + c, h * 8 + z)


def kernel(
    x_hbm, gain_hbm, shift_hbm, w1_hbm, b1_hbm, w2_hbm, b2_hbm, wf_hbm, bf_hbm, out,
    xv, gain, shift, w1, b1, w2, b2, wf, bf,
    normed0, normed1, tright, lrows, rown, rpart, lbuf, rbuf, lt, wfloat, wrows, wt, outer, obuf,
    in_sem, out_sem, lsend, lrecv, r0send, r0recv, r1send, r1recv, r2send, r2recv, r3send, r3recv,
):
    r, q = lax.axis_index("res"), lax.axis_index("seq")
    x, yl, c, h, z = r // 4, (r // 2) % 2, r % 2, q // 8, q % 8
    xp, xm, xo = (x + 1) % 4, (x + 3) % 4, (x + 2) % 4
    zp, zm = (z + 1) % 8, (z + 7) % 8
    half = (c + h + z + 1) % 2
    src_yl, src_c = (q // 2) % 2, q % 2
    piece = x * 2 + yl

    barrier = pltpu.get_barrier_semaphore()
    sources = [device(x, yl, c, h, zp), device(x, yl, c, h, zm), device(x, yl, c, 1 - h, z)]
    sources += [device(xp, yl, c, h, z), device(xm, yl, c, h, z), device(xo, yl, c, h, z)]
    sources += [device(x, 1 - yl, c, h, z), device(x, yl, 1 - c, h, z)]
    sources += [device(x, src_yl, src_c, half, k) for k in range(8)]
    for who in sources:
        pl.semaphore_signal(barrier, inc=1, device_id=who, device_id_type=MESH)

    loads = []
    for k, (src, dst) in enumerate([
        (x_hbm, xv), (gain_hbm, gain), (shift_hbm, shift), (w1_hbm, w1), (b1_hbm, b1),
        (w2_hbm, w2), (b2_hbm, b2), (wf_hbm, wf), (bf_hbm, bf),
    ]):
        for n in range(4 if k == 0 else 1):
            if k == 0:
                src, dst = x_hbm.at[pl.ds(n * 8, 8)], xv.at[pl.ds(n * 8, 8)]
            loads.append(pltpu.make_async_copy(src, dst, in_sem.at[len(loads)]))
            loads[-1].start()
    xloads, loads = loads[:4], loads[3:]
    for load in loads[1:7]:
        load.wait()

    b2c = jnp.broadcast_to(b2[...].reshape(1, HID), (128, HID)).T
    b2c = jnp.concatenate([b2c] * 4, axis=1)
    g, o = gain[...].reshape(1, CH), shift[...].reshape(1, CH)

    def norm_step(b):
        xloads[b].wait()
        v = xv[b * 8:b * 8 + 8].reshape(8 * POS, CH).astype(F32)
        d = v - jnp.mean(v, axis=-1, keepdims=True)
        n = d * lax.rsqrt(jnp.mean(d * d, axis=-1, keepdims=True) + 1e-05) * g + o
        normed0[pl.ds(b * 512, 512), :] = n[:, :128]
        normed1[pl.ds(b * 512, 512), :] = n[:, 128:]
        t = lax.dot_general(w2[...], n.astype(BF16), (((1,), (1,)), ((), ())), preferred_element_type=F32) + b2c
        for u in range(4):
            tright[pl.ds((b * 4 + u) * HID, HID), :] = t[:, u * 128:(u + 1) * 128]

    for b in range(SEQS // 8):
        norm_step(b)
    low = lax.broadcasted_iota(jnp.int32, (16, 128), 1) < POS
    for t in range(HID // 2):
        a = tright[pl.ds(2 * t, 16, stride=HID), :]
        b = tright[pl.ds(2 * t + 1, 16, stride=HID), :]
        lane = (t % 2) * 128
        rown[t // 2, 0:16, lane:lane + 128] = jnp.where(low, a, pltpu.roll(b, POS, 1)).astype(BF16)
        rown[t // 2, 16:32, lane:lane + 128] = jnp.where(low, pltpu.roll(a, POS, 1), b).astype(BF16)

    lane4 = lax.broadcasted_iota(jnp.int32, (4 * CH, 128), 1) // HID
    row4 = lax.broadcasted_iota(jnp.int32, (4 * CH, 128), 0) // CH
    w1w = jnp.concatenate([w1[...].astype(F32).T] * 4, axis=1)
    w1w = jnp.where(lane4 == row4, jnp.concatenate([w1w] * 4, axis=0), 0.0).astype(BF16)
    b1w = jnp.concatenate([b1[...].reshape(1, HID)] * 4, axis=1)

    pl.semaphore_wait(barrier, len(sources))

    pending = []

    def send(src, dst, ssem, rsem, who):
        copy = pltpu.make_async_remote_copy(
            src_ref=src, dst_ref=dst, send_sem=ssem, recv_sem=rsem, device_id=who, device_id_type=MESH
        )
        copy.start()
        pending.append(copy)

    def arrived(ref, sem):
        pltpu.make_async_remote_copy(
            src_ref=ref, dst_ref=ref, send_sem=sem, recv_sem=sem, device_id=device(x, yl, 1 - c, h, z),
            device_id_type=MESH,
        ).wait_recv()

    px, mx, ox = device(xp, yl, c, h, z), device(xm, yl, c, h, z), device(xo, yl, c, h, z)
    for n, (xx, who) in enumerate(((xp, px), (xm, mx), (xo, ox))):
        send(rown.at[pl.ds(2 * xx, 2)], rpart.at[x], r0send.at[n], r0recv.at[x], who)

    def scatter(n, xs, ref):
        hd = xs // 2
        for y2 in range(2):
            send(
                ref.at[y2], rbuf.at[2 * x + y2, q], r1send.at[2 * n + y2], r1recv.at[z],
                device(x, y2, (h + hd + c + 1) % 2, hd, (xs % 2) * 4 + yl * 2 + c),
            )

    scatter(0, x, rown.at[pl.ds(2 * x, 2)])

    def chunk(side, d):
        hh = h if side == 0 else 1 - h
        return hh * 8 + (z + d + 8) % 8

    def lsend_to(p, k, idx, who):
        send(lbuf.at[p, idx], lbuf.at[p, idx], lsend.at[p, k], lrecv.at[p, idx], who)

    def lwait(p, side, d):
        idx = chunk(side, d)
        arrived(lbuf.at[p, idx], lrecv.at[p, idx])

    up, down, over = device(x, yl, c, h, zp), device(x, yl, c, h, zm), device(x, yl, c, 1 - h, z)

    def own(p):
        for gl in range(PI // 4):
            for i4 in range(4):
                i = p * PI + gl * 4 + i4
                for lo in range(2):
                    for n, normed in enumerate((normed0, normed1)):
                        lane = i4 * CH + n * 128
                        lrows[gl * 32 + lo * 16:gl * 32 + lo * 16 + 16, lane:lane + 128] = normed[
                            pl.ds(lo * POS + i, 16, stride=2 * POS), :
                        ].astype(BF16)
        left = (jnp.dot(lrows[...], w1w, preferred_element_type=F32) + b1w).astype(BF16)
        for gl in range(PI // 4):
            lbuf[p, q, :, gl * 128:(gl + 1) * 128] = left[gl * 32:(gl + 1) * 32, :]
        lsend_to(p, 0, q, up)
        lsend_to(p, 4, q, down)
        lsend_to(p, 8, q, over)

    other = x * 2 + 1 - yl
    yld, sib = device(x, 1 - yl, c, h, z), device(x, yl, 1 - c, h, z)

    def rows(k, m):
        return rbuf.at[k, pl.ds(half * 8 + m * RG, RG)]

    def rsend(n, k, zz, who):
        send(rows(k, zz), rows(k, zz), r2send.at[n, zz], r2recv.at[k, zz], who)

    def rwait(k, zz):
        arrived(rows(k, zz), r2recv.at[k, zz])

    def eighth(k, which):
        return rbuf.at[k, pl.ds(which * 8, 8)]

    def rsibling(n, k):
        send(eighth(k, half), eighth(k, half), r3send.at[n], r3recv.at[k], sib)

    def rgather(n, k):
        for m in range(8 // RG):
            rwait(k, m)
        rsibling(n, k)

    near = {1: (0, 1, -1, 2, -2, 3, -3, 4), 2: (0, 1, -1, 2), 4: (0, 1), 8: (0,)}[RG]

    def r0():
        for n, xx in enumerate((xp, xm, xo)):
            arrived(rpart.at[xx], r0recv.at[xx])
            scatter(n + 1, xx, rpart.at[xx])

    def r1(d):
        zz = (z // RG + d + 8) % (8 // RG)
        for n in range(RG):
            arrived(rbuf.at[piece, half * 8 + zz * RG + n], r1recv.at[zz * RG + n])
        rsend(0, piece, zz, yld)
        rsend(1, piece, zz, px)
        rsend(2, piece, zz, mx)
        rsend(3, piece, zz, ox)
        if d == near[-1]:
            rsibling(0, piece)

    def ryl(d):
        zz = (z // RG + d + 8) % (8 // RG)
        rwait(other, zz)
        rsend(4, other, zz, px)
        rsend(5, other, zz, mx)
        if d == near[-1]:
            rsibling(1, other)

    def rant(d):
        zz = (z // RG + d + 8) % (8 // RG)
        rwait(xo * 2 + yl, zz)
        rsend(6, xo * 2 + yl, zz, yld)
        if d == near[-1]:
            rsibling(2, xo * 2 + yl)

    def rsib():
        for k in range(PIECES):
            arrived(eighth(k, 1 - half), r3recv.at[k])

    def weights():
        loads[7].wait()
        loads[8].wait()
        wfloat[...] = wf[...].astype(F32)
        for e in range(HID):
            wrows[(e // 2) * HID:(e // 2 + 1) * HID, (e % 2) * CZ:(e % 2 + 1) * CZ] = wfloat[pl.ds(e, HID, stride=HID), :]
        wt[...] = wrows[...].T.astype(BF16)


    def s1(p):
        lwait(p, 0, -1)
        lsend_to(p, 1, chunk(0, -1), up)
        lsend_to(p, 9, chunk(0, -1), over)
        lwait(p, 0, 1)
        lsend_to(p, 5, chunk(0, 1), down)
        lsend_to(p, 10, chunk(0, 1), over)

    def crosses(p, d):
        return CROSS[p] == 2 or CROSS[p] == 1 and (d < 0) == (p % 2 == 0)

    def s2(p):
        lwait(p, 0, -2)
        lsend_to(p, 2, chunk(0, -2), up)
        if crosses(p, -2):
            lsend_to(p, 11, chunk(0, -2), over)
        lwait(p, 0, 2)
        lsend_to(p, 6, chunk(0, 2), down)
        if crosses(p, 2):
            lsend_to(p, 16, chunk(0, 2), over)

    def s3(p):
        lwait(p, 0, -3)
        if p % 2 == 1:
            lsend_to(p, 3, chunk(0, -3), up)
        lwait(p, 0, 3)
        if p % 2 == 0:
            lsend_to(p, 7, chunk(0, 3), down)

    def c1(p):
        if not crosses(p, -2):
            lwait(p, 1, -1)
            lsend_to(p, 12, chunk(1, -1), up)
        if not crosses(p, 2):
            lwait(p, 1, 1)
            lsend_to(p, 17, chunk(1, 1), down)

    def c2(p):
        lwait(p, 1, -2)
        lsend_to(p, 13, chunk(1, -2), up)
        lwait(p, 1, 2)
        lsend_to(p, 14, chunk(1, 2), down)

    def c3(p):
        if p % 2 == 0:
            lwait(p, 1, -3)
            lsend_to(p, 15, chunk(1, -3), up)
        else:
            lwait(p, 1, 3)
            lsend_to(p, 15, chunk(1, 3), down)

    def finish(p):
        for side, d in ((0, 4), (1, 0), (1, 4), (1, 3 if p % 2 == 0 else -3)):
            lwait(p, side, d)
        for d in (-1, 1):
            if crosses(p, 2 * d):
                lwait(p, 1, d)

    low2 = lax.broadcasted_iota(jnp.int32, (128, 128), 1) < POS

    def turn(p):
        for b in range(4):
            for n in range(0, GI * HID, min(GI * HID, LANES)):
                part, lane = divmod(p * GI * HID + n, LANES)
                width = min(GI * HID, LANES)
                lt[p % 2, n:n + width, b * 128:(b + 1) * 128] = (
                    lbuf[part, 4 * b:4 * b + 4, :, lane:lane + width].reshape(128, width).T
                )

    def multiply(p, k):
        prod = jnp.dot(lt[p % 2], rbuf[k].reshape(TOTAL, 256), preferred_element_type=F32).astype(BF16)
        for i in range(GI):
            for t in range(2):
                outer[p % 2, i // 2, (2 * k + t) * HID:(2 * k + t + 1) * HID, (i % 2) * 128:(i % 2 + 1) * 128] = prod[
                    i * HID:(i + 1) * HID, t * 128:(t + 1) * 128
                ]

    def project(p, n):
        y = jnp.dot(wt[...], outer[p % 2, n], preferred_element_type=F32)
        for i in range(2):
            both = jnp.where(low2, y[:CZ, i * 128:(i + 1) * 128], y[CZ:, i * 128:(i + 1) * 128]).T
            pair = (both[:POS] + both[POS:]) * (1.0 / TOTAL) + bf[...].reshape(1, CZ)
            obuf[p * GI + 2 * n + i] = pair.astype(BF16)

    def store(p):
        copy = pltpu.make_async_copy(obuf.at[pl.ds(p * GI, GI)], out.at[pl.ds(p * GI, GI)], out_sem.at[p])
        copy.start()
        return copy


    steps = []

    def plan(start, pitch, step, items):
        for n, item in enumerate(items):
            steps.append((start + pitch * n, functools.partial(step, item)))

    steps.append((3.5, r0))
    plan(8.0 + 0.15 * (RG - 1), 0.3 * RG, r1, near)
    plan(12.0, 0.4 * RG, ryl, near)
    plan(14.0, 0.45 * RG, rant, near)
    for n, (when, k) in enumerate(((14.6, xp * 2 + yl), (14.7, xm * 2 + yl), (17.0, xp * 2 + 1 - yl), (17.1, xm * 2 + 1 - yl), (17.6, xo * 2 + 1 - yl))):
        steps.append((when, functools.partial(rgather, 3 + n, k)))
    steps.append((18.4, rsib))
    parts = range(PARTS)
    plan(0.0, 0.8 / PARTS, own, parts)
    steps.append((1.0, weights))
    pitch = 2.6 / PARTS
    plan(3.9, pitch, s1, parts)
    plan(7.0, pitch, s2, parts)
    plan(8.1, pitch, c1, parts)
    plan(10.0, pitch, s3, parts)
    plan(12.6, pitch, c2, parts)
    plan(15.5, pitch, c3, parts)
    for _, step in sorted(steps, key=lambda item: item[0]):
        step()
    stores = []
    each = GI // 2 // PIECES
    for p in range(GROUPS):
        for n in range(PARTS):
            if n * GROUPS // PARTS == p:
                finish(n)
        turn(p)
        for n in range(PIECES):
            multiply(p, n)
            if p > 0:
                for m in range(each):
                    project(p - 1, n * each + m)
        if p > 0:
            stores.append(store(p - 1))
    for n in range(GI // 2):
        project(GROUPS - 1, n)
    stores.append(store(GROUPS - 1))
    for copy in stores:
        copy.wait()
    for copy in pending:
        copy.wait_send()


def local(x, gain, shift, w1, b1, w2, b2, wf, bf):
    args = [pltpu.with_memory_space_constraint(a, pltpu.HBM) for a in (x, gain, shift, w1.T, b1, w2.T, b2, wf, bf)]
    dma = pltpu.SemaphoreType.DMA
    return pl.pallas_call(
        kernel,
        out_shape=jax.ShapeDtypeStruct((POS, POS, CZ), BF16),
        in_specs=[pl.BlockSpec(memory_space=pltpu.HBM)] * 9,
        out_specs=pl.BlockSpec(memory_space=pl.ANY),
        scratch_shapes=[
            pltpu.VMEM((SEQS, POS, CH), BF16), pltpu.VMEM((CH,), F32), pltpu.VMEM((CH,), F32),
            pltpu.VMEM((HID, CH), BF16), pltpu.VMEM((HID,), F32),
            pltpu.VMEM((HID, CH), BF16), pltpu.VMEM((HID,), F32),
            pltpu.VMEM((HID * HID, CZ), BF16), pltpu.VMEM((CZ,), F32),
            pltpu.VMEM((SEQS * POS, 128), F32), pltpu.VMEM((SEQS * POS, 128), F32),
            pltpu.VMEM((SEQS // 2 * HID, 128), F32),
            pltpu.VMEM((PI // 4 * SEQS, 4 * CH), BF16),
            pltpu.VMEM((PIECES, SEQS, 256), BF16),
            pltpu.VMEM((4, 2, SEQS, 256), BF16),
            pltpu.VMEM((PARTS, NQ, SEQS, LANES), BF16),
            pltpu.VMEM((PIECES, NQ, SEQS, 256), BF16),
            pltpu.VMEM((2, GI * HID, TOTAL), BF16),
            pltpu.VMEM((HID * HID, CZ), F32),
            pltpu.VMEM((HID * HID // 2, 2 * CZ), F32),
            pltpu.VMEM((2 * CZ, HID * HID // 2), BF16),
            pltpu.VMEM((2, GI // 2, HID * HID // 2, 256), BF16),
            pltpu.VMEM((POS, POS, CZ), BF16),
            dma((12,)), dma((GROUPS,)), dma((PARTS, 18)), dma((PARTS, NQ)), dma((3,)), dma((4,)), dma((PIECES,)), dma((8,)),
            dma((7, 8)), dma((PIECES, 8)), dma((PIECES,)), dma((PIECES,)),
        ],
        compiler_params=pltpu.CompilerParams(
            collective_id=0, has_side_effects=True, vmem_limit_bytes=40 * 2**20
        ),
    )(*args)


def solution(mesh):
    return jax.shard_map(
        local,
        mesh=mesh,
        in_specs=(P("seq", "res", None), P(), P(), P(), P(), P(), P(), P(), P()),
        out_specs=P("res", "seq", None),
        check_vma=False,
    )
```

```python
import functools

import jax
import jax.numpy as jnp
from jax import lax
from jax.experimental import pallas as pl
from jax.experimental.pallas import tpu as pltpu
from jax.sharding import PartitionSpec as P

MESH = pl.DeviceIdType.MESH
BF16, F32 = jnp.bfloat16, jnp.float32
SEQS, POS, CH, HID, CZ = 32, 64, 256, 32, 128
NQ = 16
CROSS = (0, 0, 0, 0)
RG = 2
PARTS = 4
PI = POS // PARTS
LANES = PI * HID
GROUPS = 1
GI = POS // GROUPS
PIECES = 8
TOTAL = SEQS * NQ


def device(x, yl, c, h, z):
    return (x * 4 + yl * 2 + c, h * 8 + z)


def kernel(
    x_hbm, gain_hbm, shift_hbm, w1_hbm, b1_hbm, w2_hbm, b2_hbm, wf_hbm, bf_hbm, out,
    xv, gain, shift, w1, b1, w2, b2, wf, bf,
    normed0, normed1, tright, lrows, rown, rpart, lbuf, rbuf, lt, wfloat, wrows, wt, outer,
    in_sem, lsend, lrecv, r0send, r0recv, r1send, r1recv, r2send, r2recv, r3send, r3recv,
):
    r, q = lax.axis_index("res"), lax.axis_index("seq")
    x, yl, c, h, z = r // 4, (r // 2) % 2, r % 2, q // 8, q % 8
    xp, xm, xo = (x + 1) % 4, (x + 3) % 4, (x + 2) % 4
    zp, zm = (z + 1) % 8, (z + 7) % 8
    half = (c + h + z + 1) % 2
    src_yl, src_c = (q // 2) % 2, q % 2
    piece = x * 2 + yl

    barrier = pltpu.get_barrier_semaphore()
    sources = [device(x, yl, c, h, zp), device(x, yl, c, h, zm), device(x, yl, c, 1 - h, z)]
    sources += [device(xp, yl, c, h, z), device(xm, yl, c, h, z), device(xo, yl, c, h, z)]
    sources += [device(x, 1 - yl, c, h, z), device(x, yl, 1 - c, h, z)]
    sources += [device(x, src_yl, src_c, half, k) for k in range(8)]
    for who in sources:
        pl.semaphore_signal(barrier, inc=1, device_id=who, device_id_type=MESH)

    loads = []
    for k, (src, dst) in enumerate([
        (x_hbm, xv), (gain_hbm, gain), (shift_hbm, shift), (w1_hbm, w1), (b1_hbm, b1),
        (w2_hbm, w2), (b2_hbm, b2), (wf_hbm, wf), (bf_hbm, bf),
    ]):
        for n in range(4 if k == 0 else 1):
            if k == 0:
                src, dst = x_hbm.at[pl.ds(n * 8, 8)], xv.at[pl.ds(n * 8, 8)]
            loads.append(pltpu.make_async_copy(src, dst, in_sem.at[len(loads)]))
            loads[-1].start()
    xloads, loads = loads[:4], loads[3:]
    for load in loads[1:7]:
        load.wait()

    b2c = jnp.broadcast_to(b2[...].reshape(1, HID), (128, HID)).T
    b2c = jnp.concatenate([b2c] * 4, axis=1)
    g, o = gain[...].reshape(1, CH), shift[...].reshape(1, CH)

    def norm_step(b):
        xloads[b].wait()
        v = xv[b * 8:b * 8 + 8].reshape(8 * POS, CH).astype(F32)
        d = v - jnp.mean(v, axis=-1, keepdims=True)
        n = d * lax.rsqrt(jnp.mean(d * d, axis=-1, keepdims=True) + 1e-05) * g + o
        normed0[pl.ds(b * 512, 512), :] = n[:, :128]
        normed1[pl.ds(b * 512, 512), :] = n[:, 128:]
        t = lax.dot_general(w2[...], n.astype(BF16), (((1,), (1,)), ((), ())), preferred_element_type=F32) + b2c
        for u in range(4):
            tright[pl.ds((b * 4 + u) * HID, HID), :] = t[:, u * 128:(u + 1) * 128]

    for b in range(SEQS // 8):
        norm_step(b)
    low = lax.broadcasted_iota(jnp.int32, (16, 128), 1) < POS
    for t in range(HID // 2):
        a = tright[pl.ds(2 * t, 16, stride=HID), :]
        b = tright[pl.ds(2 * t + 1, 16, stride=HID), :]
        lane = (t % 2) * 128
        rown[t // 2, 0:16, lane:lane + 128] = jnp.where(low, a, pltpu.roll(b, POS, 1)).astype(BF16)
        rown[t // 2, 16:32, lane:lane + 128] = jnp.where(low, pltpu.roll(a, POS, 1), b).astype(BF16)

    lane4 = lax.broadcasted_iota(jnp.int32, (4 * CH, 128), 1) // HID
    row4 = lax.broadcasted_iota(jnp.int32, (4 * CH, 128), 0) // CH
    w1w = jnp.concatenate([w1[...].astype(F32).T] * 4, axis=1)
    w1w = jnp.where(lane4 == row4, jnp.concatenate([w1w] * 4, axis=0), 0.0).astype(BF16)
    b1w = jnp.concatenate([b1[...].reshape(1, HID)] * 4, axis=1)

    pl.semaphore_wait(barrier, len(sources))

    pending = []

    def send(src, dst, ssem, rsem, who):
        copy = pltpu.make_async_remote_copy(
            src_ref=src, dst_ref=dst, send_sem=ssem, recv_sem=rsem, device_id=who, device_id_type=MESH
        )
        copy.start()
        pending.append(copy)

    def arrived(ref, sem):
        pltpu.make_async_remote_copy(
            src_ref=ref, dst_ref=ref, send_sem=sem, recv_sem=sem, device_id=device(x, yl, 1 - c, h, z),
            device_id_type=MESH,
        ).wait_recv()

    px, mx, ox = device(xp, yl, c, h, z), device(xm, yl, c, h, z), device(xo, yl, c, h, z)
    for n, (xx, who) in enumerate(((xp, px), (xm, mx), (xo, ox))):
        send(rown.at[pl.ds(2 * xx, 2)], rpart.at[x], r0send.at[n], r0recv.at[x], who)

    def scatter(n, xs, ref):
        hd = xs // 2
        for y2 in range(2):
            send(
                ref.at[y2], rbuf.at[2 * x + y2, q], r1send.at[2 * n + y2], r1recv.at[z],
                device(x, y2, (h + hd + c + 1) % 2, hd, (xs % 2) * 4 + yl * 2 + c),
            )

    scatter(0, x, rown.at[pl.ds(2 * x, 2)])

    def chunk(side, d):
        hh = h if side == 0 else 1 - h
        return hh * 8 + (z + d + 8) % 8

    def lsend_to(p, k, idx, who):
        send(lbuf.at[p, idx], lbuf.at[p, idx], lsend.at[p, k], lrecv.at[p, idx], who)

    def lwait(p, side, d):
        idx = chunk(side, d)
        arrived(lbuf.at[p, idx], lrecv.at[p, idx])

    up, down, over = device(x, yl, c, h, zp), device(x, yl, c, h, zm), device(x, yl, c, 1 - h, z)

    def own(p):
        for gl in range(PI // 4):
            for i4 in range(4):
                i = p * PI + gl * 4 + i4
                for lo in range(2):
                    for n, normed in enumerate((normed0, normed1)):
                        lane = i4 * CH + n * 128
                        lrows[gl * 32 + lo * 16:gl * 32 + lo * 16 + 16, lane:lane + 128] = normed[
                            pl.ds(lo * POS + i, 16, stride=2 * POS), :
                        ].astype(BF16)
        left = (jnp.dot(lrows[...], w1w, preferred_element_type=F32) + b1w).astype(BF16)
        for gl in range(PI // 4):
            lbuf[p, q, :, gl * 128:(gl + 1) * 128] = left[gl * 32:(gl + 1) * 32, :]
        lsend_to(p, 0, q, up)
        lsend_to(p, 4, q, down)
        lsend_to(p, 8, q, over)

    other = x * 2 + 1 - yl
    yld, sib = device(x, 1 - yl, c, h, z), device(x, yl, 1 - c, h, z)

    def rows(k, m):
        return rbuf.at[k, pl.ds(half * 8 + m * RG, RG)]

    def rsend(n, k, zz, who):
        send(rows(k, zz), rows(k, zz), r2send.at[n, zz], r2recv.at[k, zz], who)

    def rwait(k, zz):
        arrived(rows(k, zz), r2recv.at[k, zz])

    def eighth(k, which):
        return rbuf.at[k, pl.ds(which * 8, 8)]

    def rsibling(n, k):
        send(eighth(k, half), eighth(k, half), r3send.at[n], r3recv.at[k], sib)

    def rgather(n, k):
        for m in range(8 // RG):
            rwait(k, m)
        rsibling(n, k)

    near = {1: (0, 1, -1, 2, -2, 3, -3, 4), 2: (0, 1, -1, 2), 4: (0, 1), 8: (0,)}[RG]

    def r0():
        for n, xx in enumerate((xp, xm, xo)):
            arrived(rpart.at[xx], r0recv.at[xx])
            scatter(n + 1, xx, rpart.at[xx])

    def r1(d):
        zz = (z // RG + d + 8) % (8 // RG)
        for n in range(RG):
            arrived(rbuf.at[piece, half * 8 + zz * RG + n], r1recv.at[zz * RG + n])
        rsend(0, piece, zz, yld)
        rsend(1, piece, zz, px)
        rsend(2, piece, zz, mx)
        rsend(3, piece, zz, ox)
        if d == near[-1]:
            rsibling(0, piece)

    def ryl(d):
        zz = (z // RG + d + 8) % (8 // RG)
        rwait(other, zz)
        rsend(4, other, zz, px)
        rsend(5, other, zz, mx)
        if d == near[-1]:
            rsibling(1, other)

    def rant(d):
        zz = (z // RG + d + 8) % (8 // RG)
        rwait(xo * 2 + yl, zz)
        rsend(6, xo * 2 + yl, zz, yld)
        if d == near[-1]:
            rsibling(2, xo * 2 + yl)

    def rsib():
        for k in range(PIECES):
            arrived(eighth(k, 1 - half), r3recv.at[k])

    def weights():
        loads[7].wait()
        loads[8].wait()
        wfloat[...] = wf[...].astype(F32)
        for e in range(HID):
            wrows[(e // 2) * HID:(e // 2 + 1) * HID, (e % 2) * CZ:(e % 2 + 1) * CZ] = wfloat[pl.ds(e, HID, stride=HID), :]
        wt[...] = wrows[...].T.astype(BF16)


    def s1(p):
        lwait(p, 0, -1)
        lsend_to(p, 1, chunk(0, -1), up)
        lsend_to(p, 9, chunk(0, -1), over)
        lwait(p, 0, 1)
        lsend_to(p, 5, chunk(0, 1), down)
        lsend_to(p, 10, chunk(0, 1), over)

    def crosses(p, d):
        return CROSS[p] == 2 or CROSS[p] == 1 and (d < 0) == (p % 2 == 0)

    def s2(p):
        lwait(p, 0, -2)
        lsend_to(p, 2, chunk(0, -2), up)
        if crosses(p, -2):
            lsend_to(p, 11, chunk(0, -2), over)
        lwait(p, 0, 2)
        lsend_to(p, 6, chunk(0, 2), down)
        if crosses(p, 2):
            lsend_to(p, 16, chunk(0, 2), over)

    def s3(p):
        lwait(p, 0, -3)
        if p % 2 == 1:
            lsend_to(p, 3, chunk(0, -3), up)
        lwait(p, 0, 3)
        if p % 2 == 0:
            lsend_to(p, 7, chunk(0, 3), down)

    def c1(p):
        if not crosses(p, -2):
            lwait(p, 1, -1)
            lsend_to(p, 12, chunk(1, -1), up)
        if not crosses(p, 2):
            lwait(p, 1, 1)
            lsend_to(p, 17, chunk(1, 1), down)

    def c2(p):
        lwait(p, 1, -2)
        lsend_to(p, 13, chunk(1, -2), up)
        lwait(p, 1, 2)
        lsend_to(p, 14, chunk(1, 2), down)

    def c3(p):
        if p % 2 == 0:
            lwait(p, 1, -3)
            lsend_to(p, 15, chunk(1, -3), up)
        else:
            lwait(p, 1, 3)
            lsend_to(p, 15, chunk(1, 3), down)

    def finish(p):
        for side, d in ((0, 4), (1, 0), (1, 4), (1, 3 if p % 2 == 0 else -3)):
            lwait(p, side, d)
        for d in (-1, 1):
            if crosses(p, 2 * d):
                lwait(p, 1, d)

    low2 = lax.broadcasted_iota(jnp.int32, (128, 128), 1) < POS

    def turn(p):
        for b in range(4):
            for n in range(0, GI * HID, min(GI * HID, LANES)):
                part, lane = divmod(p * GI * HID + n, LANES)
                width = min(GI * HID, LANES)
                lt[p % 2, n:n + width, b * 128:(b + 1) * 128] = (
                    lbuf[part, 4 * b:4 * b + 4, :, lane:lane + width].reshape(128, width).T
                )

    def multiply(p, k):
        prod = jnp.dot(lt[p % 2], rbuf[k].reshape(TOTAL, 256), preferred_element_type=F32).astype(BF16)
        for i in range(GI):
            for t in range(2):
                outer[p % 2, i // 2, (2 * k + t) * HID:(2 * k + t + 1) * HID, (i % 2) * 128:(i % 2 + 1) * 128] = prod[
                    i * HID:(i + 1) * HID, t * 128:(t + 1) * 128
                ]

    def project(p, n):
        y = jnp.dot(wt[...], outer[p % 2, n], preferred_element_type=F32)
        for i in range(2):
            both = jnp.where(low2, y[:CZ, i * 128:(i + 1) * 128], y[CZ:, i * 128:(i + 1) * 128]).T
            pair = (both[:POS] + both[POS:]) * (1.0 / TOTAL) + bf[...].reshape(1, CZ)
            out[p * GI + 2 * n + i] = pair.astype(BF16)


    steps = []

    def plan(start, pitch, step, items):
        for n, item in enumerate(items):
            steps.append((start + pitch * n, functools.partial(step, item)))

    steps.append((3.5, r0))
    plan(8.0 + 0.15 * (RG - 1), 0.3 * RG, r1, near)
    plan(12.0, 0.4 * RG, ryl, near)
    plan(14.0, 0.45 * RG, rant, near)
    for n, (when, k) in enumerate(((14.6, xp * 2 + yl), (14.7, xm * 2 + yl), (17.0, xp * 2 + 1 - yl), (17.1, xm * 2 + 1 - yl), (17.6, xo * 2 + 1 - yl))):
        steps.append((when, functools.partial(rgather, 3 + n, k)))
    steps.append((18.4, rsib))
    parts = range(PARTS)
    plan(0.0, 0.8 / PARTS, own, parts)
    steps.append((1.0, weights))
    pitch = 2.6 / PARTS
    plan(3.9, pitch, s1, parts)
    plan(7.0, pitch, s2, parts)
    plan(8.1, pitch, c1, parts)
    plan(10.0, pitch, s3, parts)
    plan(12.6, pitch, c2, parts)
    plan(15.5, pitch, c3, parts)
    for _, step in sorted(steps, key=lambda item: item[0]):
        step()
    each = GI // 2 // PIECES
    for p in range(GROUPS):
        for n in range(PARTS):
            if n * GROUPS // PARTS == p:
                finish(n)
        turn(p)
        for n in range(PIECES):
            multiply(p, n)
            if p > 0:
                for m in range(each):
                    project(p - 1, n * each + m)
    for n in range(GI // 2):
        project(GROUPS - 1, n)
    for copy in pending:
        copy.wait_send()


def local(x, gain, shift, w1, b1, w2, b2, wf, bf):
    args = [pltpu.with_memory_space_constraint(a, pltpu.HBM) for a in (x, gain, shift, w1.T, b1, w2.T, b2, wf, bf)]
    dma = pltpu.SemaphoreType.DMA
    return pl.pallas_call(
        kernel,
        out_shape=jax.ShapeDtypeStruct((POS, POS, CZ), BF16),
        in_specs=[pl.BlockSpec(memory_space=pltpu.HBM)] * 9,
        out_specs=pl.BlockSpec(memory_space=pltpu.VMEM),
        scratch_shapes=[
            pltpu.VMEM((SEQS, POS, CH), BF16), pltpu.VMEM((CH,), F32), pltpu.VMEM((CH,), F32),
            pltpu.VMEM((HID, CH), BF16), pltpu.VMEM((HID,), F32),
            pltpu.VMEM((HID, CH), BF16), pltpu.VMEM((HID,), F32),
            pltpu.VMEM((HID * HID, CZ), BF16), pltpu.VMEM((CZ,), F32),
            pltpu.VMEM((SEQS * POS, 128), F32), pltpu.VMEM((SEQS * POS, 128), F32),
            pltpu.VMEM((SEQS // 2 * HID, 128), F32),
            pltpu.VMEM((PI // 4 * SEQS, 4 * CH), BF16),
            pltpu.VMEM((PIECES, SEQS, 256), BF16),
            pltpu.VMEM((4, 2, SEQS, 256), BF16),
            pltpu.VMEM((PARTS, NQ, SEQS, LANES), BF16),
            pltpu.VMEM((PIECES, NQ, SEQS, 256), BF16),
            pltpu.VMEM((2, GI * HID, TOTAL), BF16),
            pltpu.VMEM((HID * HID, CZ), F32),
            pltpu.VMEM((HID * HID // 2, 2 * CZ), F32),
            pltpu.VMEM((2 * CZ, HID * HID // 2), BF16),
            pltpu.VMEM((2, GI // 2, HID * HID // 2, 256), BF16),
            dma((12,)), dma((PARTS, 18)), dma((PARTS, NQ)), dma((3,)), dma((4,)), dma((PIECES,)), dma((8,)),
            dma((7, 8)), dma((PIECES, 8)), dma((PIECES,)), dma((PIECES,)),
        ],
        compiler_params=pltpu.CompilerParams(
            collective_id=0, has_side_effects=True, vmem_limit_bytes=40 * 2**20
        ),
    )(*args)


def solution(mesh):
    return jax.shard_map(
        local,
        mesh=mesh,
        in_specs=(P("seq", "res", None), P(), P(), P(), P(), P(), P(), P(), P()),
        out_specs=P("res", "seq", None),
        check_vma=False,
    )
```
